128 devices in a mesh: gx: 8 (over z, core), gy: 16 (over x, y).
Axes of the slice: x: 4, y: 4, z: 4, core: 2. Of those that a mesh axis runs over, the one named last changes fastest.
Arguments:
- field: float32 [32, 4096, 4096], P(None, 'gx', 'gy'), may hold values from -6 to 6
- mode2_factor: float32 [4096, 64], P('gy'), may hold values from -0.09375 to 0.09375
- mode3_factor: float32 [32, 16], replicated, may hold values from -1 to 1
- start_factor: float32 [4096, 64], P('gx'), may hold values from -0.09375 to 0.09375
Outputs:
- new_factor: float32 [4096, 64], P('gx')
The draws below stay inside these ranges and needn't reach their ends.
All inputs are finite; a program needn't handle non-finite values.
Results may differ from the reference program's by a relative error of at most 0.0003.
Values sent between devices are 32-bit elements; how exact they have to be, the bound alone decides.
A program may use at most 64 MiB of HBM per device.

```python
import math
import jax
import jax.numpy as jnp
from jax import lax

T3 = 32
R1 = 64
R2 = 64
R3 = 16
ITERS = 2
N1 = 4096
N2 = 4096


def block_levels(stream_key, dims, pieces, smallest, top_value):
    def one(position, shards_of):
        steps = jax.random.uniform(jax.random.fold_in(jax.random.fold_in(stream_key, 6), position), (shards_of,), jnp.float32, smallest / len(pieces), top_value / len(pieces))
        return jnp.repeat(jnp.exp(steps), dims[position] // shards_of).reshape((-1,) + (1,) * (len(dims) - position - 1))

    gain = one(*pieces[0])
    for cut in pieces[1:]:
        gain = gain * one(*cut)
    return gain


def bell_draw(key, shape, spread, most, split=(), held_as=jnp.bfloat16):
    gain = block_levels(key, shape, split, -0.22, 0.18) if split else 1.0
    array = jax.random.normal(key, shape, jnp.float32) * spread * gain
    return jnp.minimum(jnp.maximum(array, -most), most).astype(held_as)


def setup_inputs(seed: int = 0) -> dict:
    key_list = jax.random.split(jax.random.key(seed), 5)
    return {
        "field": bell_draw(key_list[0], (T3, N1, N2), 1.0, 6.0, ((1, 8), (2, 16)), jnp.float32),
        "mode2_factor": bell_draw(key_list[1], (N2, R2), N2 ** -0.5, 0.09375, ((0, 16),), jnp.float32),
        "mode3_factor": bell_draw(key_list[2], (T3, R3), T3 ** -0.5, 1.0, (), jnp.float32),
        "start_factor": bell_draw(key_list[3], (N1, R1), N1 ** -0.5, 0.09375, ((0, 8),), jnp.float32),
    }


HIGH = lax.Precision.HIGHEST

def reference(field, mode2_factor, mode3_factor, start_factor):
    block = math.gcd(N1, 64)

    def project(index):
        piece = lax.dynamic_slice_in_dim(field, (index * block).astype(jnp.int32), block, 1)
        timed = jnp.einsum('tab,ts->sab', piece, mode3_factor, precision=HIGH)
        part = jnp.einsum('sab,bq->aqs', timed, mode2_factor, precision=HIGH)
        return part.reshape(block, R2 * R3)
    unfolded = lax.map(project, jnp.arange(N1 // block, dtype=jnp.int32)).reshape(N1, R2 * R3)
    basis = start_factor
    for step in range(ITERS):
        left = jnp.dot(unfolded.T, basis, precision=HIGH)
        image = jnp.dot(unfolded, left, precision=HIGH)
        gram = jnp.dot(image.T, image, precision=HIGH)
        lower = jnp.linalg.cholesky(gram)
        basis = lax.linalg.triangular_solve(lower, image, left_side=False, lower=True, transpose_a=True)
    return basis * jnp.sqrt(jnp.float32(N1))
```

```python
import jax
import jax.numpy as jnp
from jax import lax
from jax.experimental import pallas as pl
from jax.experimental.pallas import tpu as pltpu
from jax.sharding import PartitionSpec as P

MESH = pl.DeviceIdType.MESH
HIGH = lax.Precision.HIGHEST
F32 = jnp.float32
BF16 = jnp.bfloat16

T3 = 32
R3 = 16
RANK = 64
ROWS = 512
COLS = 256
GX = 8
GY = 16
CHUNKS = 8
CHUNK = ROWS // CHUNKS
PACKED = ROWS // 2
SHARE = PACKED // GY
NN = (((1,), (0,)), ((), ()))
NT = (((1,), (1,)), ((), ()))
TN = (((0,), (0,)), ((), ()))


def dot(a, b, dims=NN):
    return lax.dot_general(a, b, dims, precision=HIGH, preferred_element_type=F32)


def bdot(a, b):
    return lax.dot_general(a, b, NN, preferred_element_type=F32)


def split(a):
    high = a.astype(BF16)
    return high, (a - high.astype(F32)).astype(BF16)


def swap(a):
    return pltpu.roll(a, 64, 1)


def lower_lanes(shape):
    return lax.broadcasted_iota(jnp.int32, shape, 1) < 64


def fold(m):
    return m[:64] + swap(m[64:])


def pair_up(s):
    return jnp.where(lower_lanes((32, 128)), s[:32], swap(s[32:]))


def unpair(p):
    return jnp.concatenate([p, swap(p)], axis=0)


def twice(s):
    low = lower_lanes((64, 128))
    zero = jnp.zeros_like(s)
    return jnp.concatenate([jnp.where(low, s, zero), jnp.where(low, zero, swap(s))], axis=0)


def inverse_factor(gram):
    lane = lax.broadcasted_iota(jnp.int32, (8, 128), 1)
    row = lax.broadcasted_iota(jnp.int32, (8, 128), 0)
    tiles = []
    for b in range(8):
        unit = jnp.where(lane == row + (64 + 8 * b), 1.0, 0.0)
        tiles.append(jnp.where(lane < 64, gram[8 * b : 8 * b + 8], unit))
    for k in range(64):
        own, at = divmod(k, 8)
        line = tiles[own][at : at + 1]
        scaled = line * (1.0 / line[:, k : k + 1])
        for b in range(own, 8):
            col = tiles[b][:, k : k + 1]
            if b == own:
                col = jnp.where(row[:, :1] > at, col, 0.0)
            tiles[b] = tiles[b] - col * scaled
    out = []
    for b in range(8):
        diag = jnp.sum(jnp.where(lane == row + 8 * b, tiles[b], 0.0), axis=1, keepdims=True)
        out.append(tiles[b] * lax.rsqrt(diag))
    return swap(jnp.concatenate(out, axis=0))


def kernel(
    field_hbm, m2_hbm, m3_hbm, start_hbm, out_ref,
    field, m2, m3, start,
    part, got, pair, basis, left_out, left_in, image, share_in, share, full,
    in_sem, small_sem, rs_send, rs_recv, x_send, x_recv, s_send, s_recv, g_send, g_recv,
):
    mx = lax.axis_index("gx")
    my = lax.axis_index("gy")

    small = [
        pltpu.make_async_copy(src, dst, small_sem.at[n])
        for n, (src, dst) in enumerate(((m2_hbm, m2), (m3_hbm, m3), (start_hbm, start)))
    ]
    loads = [
        pltpu.make_async_copy(
            field_hbm.at[:, pl.ds(c * CHUNK, CHUNK), :],
            field.at[:, pl.ds(c * CHUNK, CHUNK), :],
            in_sem.at[c],
        )
        for c in range(CHUNKS)
    ]
    small[0].start()
    small[1].start()
    for copy in loads:
        copy.start()
    small[2].start()

    barrier = pltpu.get_barrier_semaphore()

    @pl.loop(1, GY)
    def _(r):
        pl.semaphore_signal(barrier, inc=1, device_id={"gy": lax.rem(my + r, GY)}, device_id_type=MESH)

    @pl.loop(1, GX)
    def _(r):
        pl.semaphore_signal(barrier, inc=1, device_id={"gx": lax.rem(mx + r, GX)}, device_id_type=MESH)

    small[0].wait()
    small[1].wait()
    m2h, m2l = split(m2[...])
    right = jnp.concatenate([m2h, m2l], axis=1)
    tall = jnp.where(
        lax.broadcasted_iota(jnp.int32, (128, R3), 0) // 8 == lax.broadcasted_iota(jnp.int32, (128, R3), 1), 1.0, 0.0
    )
    wide = jnp.where(
        lax.broadcasted_iota(jnp.int32, (T3, 256), 0) == lax.broadcasted_iota(jnp.int32, (T3, 256), 1) // 8, 1.0, 0.0
    )
    spread = dot(dot(tall, m3[...], NT), wide)
    same = (
        lax.broadcasted_iota(jnp.int32, (128, 256), 0) % 8 == lax.broadcasted_iota(jnp.int32, (128, 256), 1) % 8
    )
    wh, wl = split(jnp.where(same, spread, 0.0))
    w2 = jnp.concatenate([wh, wl], axis=0)
    low = lower_lanes((128, 128))

    def project(i0):
        tile = field[:, pl.ds(i0, 8), :].reshape(T3 * 8, COLS)
        th, tl = split(tile)
        return bdot(th, right) + bdot(tl, right)

    for c in range(CHUNKS):
        loads[c].wait()

        @pl.loop(0, CHUNK // 16)
        def _(n):
            i0 = pl.multiple_of(c * CHUNK + n * 16, 16)
            both = jnp.concatenate([project(i0), project(i0 + 8)], axis=1)
            bh, bl = split(both)
            two = bdot(w2, bh)
            res = two[:128] + two[128:] + bdot(wh, bl)
            a, b = res[:, :128], res[:, 128:]
            done = jnp.where(low, a + swap(a), b + swap(b))
            part[:, pl.ds(pl.multiple_of(i0 // 2, 8), 8), :] = done.reshape(R3, 8, 128)

        if c == 0:
            pl.semaphore_wait(barrier, GX + GY - 2)

        @pl.loop(1, GY)
        def _(r):
            dest = lax.rem(my + r, GY)
            at = pl.ds(c * (CHUNK // 2), CHUNK // 2)
            pltpu.make_async_remote_copy(
                part.at[dest, at], got.at[r - 1, at], rs_send, rs_recv,
                device_id={"gy": dest}, device_id_type=MESH,
            ).start()

    small[2].wait()
    halves = start[...].reshape(ROWS // 16, 2, 8, RANK)
    basis[...] = jnp.concatenate([halves[:, 0], halves[:, 1]], axis=2).reshape(PACKED, 128)

    pltpu.make_async_copy(got, got, rs_recv).wait()
    own = part[my]
    for r in range(GY - 1):
        own = own + got[r]
    pair[...] = own
    pltpu.make_async_copy(got, got, rs_send).wait()

    def sum_over_gx(n, rows, value):
        src = left_out.at[n, pl.ds(0, rows)]
        dst = left_in.at[n, :, pl.ds(0, rows)]
        src[...] = value

        @pl.loop(1, GX)
        def _(r):
            pltpu.make_async_remote_copy(
                src, left_in.at[n, r - 1, pl.ds(0, rows)], x_send.at[n], x_recv.at[n],
                device_id={"gx": lax.rem(mx + r, GX)}, device_id_type=MESH,
            ).start()

        pltpu.make_async_copy(dst, dst, x_recv.at[n]).wait()
        total = value
        for r in range(GX - 1):
            total = total + left_in[n, r, :rows]
        return total, lambda: pltpu.make_async_copy(dst, dst, x_send.at[n]).wait()

    def sum_over_gy(n, value, beside):
        image[n] = value

        @pl.loop(1, GY)
        def _(r):
            dest = lax.rem(my + r, GY)
            pltpu.make_async_remote_copy(
                image.at[n, pl.ds(pl.multiple_of(dest * SHARE, SHARE), SHARE)], share_in.at[n, r - 1],
                s_send.at[n], s_recv.at[n], device_id={"gy": dest}, device_id_type=MESH,
            ).start()

        pltpu.make_async_copy(share_in.at[n], share_in.at[n], s_recv.at[n]).wait()
        total = image[n, pl.ds(pl.multiple_of(my * SHARE, SHARE), SHARE)]
        for r in range(GY - 1):
            total = total + share_in[n, r]
        share[n] = total
        full[n, my] = total

        @pl.loop(1, GY)
        def _(r):
            pltpu.make_async_remote_copy(
                share.at[n], full.at[n, my], g_send.at[n], g_recv.at[n],
                device_id={"gy": lax.rem(my + r, GY)}, device_id_type=MESH,
            ).start()

        aside = beside()
        pltpu.make_async_copy(share_in.at[n], share_in.at[n], g_recv.at[n]).wait()

        def end():
            pltpu.make_async_copy(share_in.at[n], share_in.at[n], s_send.at[n]).wait()
            pltpu.make_async_copy(share_in.at[n], share_in.at[n], g_send.at[n]).wait()

        return full[n].reshape(PACKED, 128), aside, end

    low64 = lower_lanes((64, 128))
    total, end0 = sum_over_gx(0, 32, pair_up(fold(dot(pair[...], basis[...], TN))))
    image1, _, end1 = sum_over_gy(0, dot(pair[...], twice(unpair(total))), lambda: None)
    left = fold(dot(pair[...], image1, TN))
    gram = fold(dot(image1, image1, TN))
    total, end2 = sum_over_gx(1, 64, jnp.where(low64, left, swap(gram)))
    raw, factor, end3 = sum_over_gy(
        1, dot(pair[...], twice(total)), lambda: inverse_factor(swap(total))
    )
    image2 = dot(raw, twice(factor), NT)
    gram = fold(dot(image2, image2, TN))
    total, end4 = sum_over_gx(2, 32, pair_up(gram))
    factor = inverse_factor(unpair(total))
    final = dot(image2, twice(factor), NT) * jnp.sqrt(F32(ROWS * GX))
    final = final.reshape(ROWS // 16, 8, 128)
    for h in range(2):
        out_ref[:, h] = final[:, :, 64 * h : 64 * h + 64]
    for end in (end0, end1, end2, end3, end4):
        end()


def on_device(field, mode2_factor, mode3_factor, start_factor):
    dma = pltpu.SemaphoreType.DMA
    out = pl.pallas_call(
        kernel,
        out_shape=jax.ShapeDtypeStruct((ROWS // 16, 2, 8, RANK), F32),
        in_specs=[pl.BlockSpec(memory_space=pl.ANY)] * 4,
        out_specs=pl.BlockSpec(memory_space=pltpu.VMEM),
        scratch_shapes=[
            pltpu.VMEM((T3, ROWS, COLS), F32),
            pltpu.VMEM((COLS, RANK), F32),
            pltpu.VMEM((T3, R3), F32),
            pltpu.VMEM((ROWS, RANK), F32),
            pltpu.VMEM((R3, PACKED, 128), F32),
            pltpu.VMEM((GY - 1, PACKED, 128), F32),
            pltpu.VMEM((PACKED, 128), F32),
            pltpu.VMEM((PACKED, 128), F32),
            pltpu.VMEM((3, 64, 128), F32),
            pltpu.VMEM((3, GX - 1, 64, 128), F32),
            pltpu.VMEM((2, PACKED, 128), F32),
            pltpu.VMEM((2, GY - 1, SHARE, 128), F32),
            pltpu.VMEM((2, SHARE, 128), F32),
            pltpu.VMEM((2, GY, SHARE, 128), F32),
            dma((CHUNKS,)),
            dma((3,)),
            dma, dma,
            dma((3,)), dma((3,)),
            dma((2,)), dma((2,)),
            dma((2,)), dma((2,)),
        ],
        compiler_params=pltpu.CompilerParams(
            collective_id=0, has_side_effects=True, vmem_limit_bytes=48 * 1024 * 1024
        ),
    )(field, mode2_factor, mode3_factor, start_factor)
    return out.reshape(ROWS, RANK)


def solution(mesh):
    placed = (P(None, "gx", "gy"), P("gy", None), P(), P("gx", None))
    return jax.shard_map(
        on_device, mesh=mesh, in_specs=placed, out_specs=P("gx", None), check_vma=False
    )
```

```python
import jax
import jax.numpy as jnp
from jax import lax
from jax.experimental import pallas as pl
from jax.experimental.pallas import tpu as pltpu
from jax.sharding import PartitionSpec as P

MESH = pl.DeviceIdType.MESH
HIGH = lax.Precision.HIGHEST
F32 = jnp.float32
BF16 = jnp.bfloat16

T3 = 32
R3 = 16
RANK = 64
ROWS = 512
COLS = 256
GX = 8
GY = 16
CHUNKS = 8
HALF = ROWS // CHUNKS // 2
RING = CHUNKS
LAG = 3
EARLY = 2
STEP = 4
ROUNDS = 4
SIDE = 4
PACKED = ROWS // 2
SHARE = 128 // GY
NN = (((1,), (0,)), ((), ()))
NT = (((1,), (1,)), ((), ()))


def dot(a, b, dims=NN):
    return lax.dot_general(a, b, dims, precision=HIGH, preferred_element_type=F32)


def bdot(a, b):
    return lax.dot_general(a, b, NN, preferred_element_type=F32)


def split(a):
    high = a.astype(BF16)
    return high, (a - high.astype(F32)).astype(BF16)


def swap(a):
    return pltpu.roll(a, 64, 1)


def lower_lanes(shape):
    return lax.broadcasted_iota(jnp.int32, shape, 1) < 64


def fold(m):
    return m[:64] + swap(m[64:])


def pair_up(s):
    return jnp.where(lower_lanes((32, 128)), s[:32], swap(s[32:]))


def unpair(p):
    return jnp.concatenate([p, swap(p)], axis=0)


def twice(s):
    low = lower_lanes((64, 128))
    zero = jnp.zeros_like(s)
    return jnp.concatenate([jnp.where(low, s, zero), jnp.where(low, zero, swap(s))], axis=0)


def inverse_factor(gram):
    lane = lax.broadcasted_iota(jnp.int32, (8, 128), 1)
    row = lax.broadcasted_iota(jnp.int32, (8, 128), 0)
    tiles = []
    for b in range(8):
        unit = jnp.where(lane == row + (64 + 8 * b), 1.0, 0.0)
        tiles.append(jnp.where(lane < 64, gram[8 * b : 8 * b + 8], unit))
    wide = lambda a: jnp.broadcast_to(a, (8, 128))
    for k in range(0, 64, STEP):
        own, at = divmod(k, 8)
        lines = [wide(tiles[own][at + j : at + j + 1]) for j in range(STEP)]
        cols = [[wide(t[:, k + j : k + j + 1]) for t in tiles[own:]] for j in range(STEP)]
        entry = [[wide(cols[j][0][at + n : at + n + 1]) if n >= j else None for n in range(STEP)] for j in range(STEP)]
        for j in range(STEP):
            inverse = 1.0 / entry[j][j]
            for n in range(j + 1, STEP):
                ratio = entry[j][n] * inverse
                for i in range(n, STEP):
                    entry[n][i] = entry[n][i] - ratio * entry[j][i]
                lines[n] = lines[n] - ratio * lines[j]
                cols[n] = [c - ratio * d for c, d in zip(cols[n], cols[j])]
            scaled = lines[j] * inverse
            for b in range(own, 8):
                col = cols[j][b - own]
                if b == own:
                    col = jnp.where(row > at + j, col, 0.0)
                tiles[b] = tiles[b] - col * scaled
    out = []
    for b in range(8):
        diag = jnp.sum(jnp.where(lane == row + 8 * b, tiles[b], 0.0), axis=1, keepdims=True)
        out.append(tiles[b] * lax.rsqrt(diag))
    return swap(jnp.concatenate(out, axis=0))


def kernel(
    field_hbm, m2_hbm, m3_hbm, start_hbm, out_ref,
    field, m2, m3, start,
    part, r1, r2, r3, pair, left_out, left_in, image, share_in, share, full,
    in_sem, small_sem, ring_send, ring_recv, ready, x_send, x_recv, s_send, s_recv, g_send, g_recv,
):
    mx = lax.axis_index("gx")
    my = lax.axis_index("gy")

    small = [
        pltpu.make_async_copy(src, dst, small_sem.at[n])
        for n, (src, dst) in enumerate(((m2_hbm, m2), (m3_hbm, m3), (start_hbm, start)))
    ]
    def load(c, h):
        at = pl.ds(pl.multiple_of(h * PACKED + c * HALF, HALF), HALF)
        return pltpu.make_async_copy(field_hbm.at[:, at, :], field.at[:, at, :], in_sem.at[c, h])

    small[0].start()
    small[1].start()
    for c in range(CHUNKS):
        for h in range(2):
            load(c, h).start()
    small[2].start()

    barrier = pltpu.get_barrier_semaphore()

    px, py = my // SIDE, lax.rem(my, SIDE)
    near_all = [{"gy": lax.rem(px + d, SIDE) * SIDE + py} for d in (1, 3)]
    near_all += [{"gy": px * SIDE + lax.rem(py + d, SIDE)} for d in (1, 3)]
    near_all += [{"gx": lax.rem(mx + d, GX)} for d in (2, 6)]
    near_all += [{"gx": mx + 1 - 2 * lax.rem(mx, 2)}]

    def greet(n):
        for device in near_all:
            pl.semaphore_signal(
                barrier if n == 0 else ready.at[n - 1], inc=1, device_id=device, device_id_type=MESH
            )

    def met(n):
        pl.semaphore_wait(barrier if n == 0 else ready.at[n - 1], len(near_all))

    greet(0)

    small[0].wait()
    small[1].wait()
    m2h, m2l = split(jnp.transpose(m2[...]))
    right = jnp.concatenate([m2h, m2l], axis=1)
    tall = jnp.where(
        lax.broadcasted_iota(jnp.int32, (128, R3), 0) // 8 == lax.broadcasted_iota(jnp.int32, (128, R3), 1), 1.0, 0.0
    )
    wide = jnp.where(
        lax.broadcasted_iota(jnp.int32, (T3, 256), 0) == lax.broadcasted_iota(jnp.int32, (T3, 256), 1) // 8, 1.0, 0.0
    )
    spread = dot(dot(tall, m3[...]), wide)
    same = (
        lax.broadcasted_iota(jnp.int32, (128, 256), 0) % 8 == lax.broadcasted_iota(jnp.int32, (128, 256), 1) % 8
    )
    wh, wl = split(jnp.where(same, spread, 0.0))
    w2 = jnp.concatenate([wh, wl], axis=0)
    low = lower_lanes((256, 128))

    def project(i0):
        tile = field[:, pl.ds(i0, 8), :].reshape(T3 * 8, COLS)
        th, tl = split(tile)
        return bdot(th, right) + bdot(tl, right)

    def compute(c):
        pairs = []
        for h in range(2):
            load(c, h).wait()
        for n in range(HALF // 8):
            i0 = pl.multiple_of(c * HALF + n * 8, 8)
            a, b = project(i0), project(i0 + PACKED)
            pairs.append(jnp.where(low, a + swap(a), b + swap(b)))
        blocks = []
        for n in range(0, HALF // 8, 2):
            bh, bl = split(jnp.concatenate(pairs[n : n + 2], axis=1))
            two = bdot(w2, bh)
            res = two[:128] + two[128:] + bdot(wh, bl)
            blocks += [res[:, :128].reshape(R3, 8, 128), res[:, 128:].reshape(R3, 8, 128)]
        return blocks

    first, second = (px, py), (py, px)

    def near(half, phase, step):
        if (half + phase) % 2 == 0:
            return {"gy": lax.rem(px + step + SIDE, SIDE) * SIDE + py}
        return {"gy": px * SIDE + lax.rem(py + step + SIDE, SIDE)}

    def send(src, dst, stage, c, half, phase, step):
        pltpu.make_async_remote_copy(
            src, dst.at[c, half, (1 - step) // 2], ring_send.at[stage], ring_recv.at[stage, c],
            device_id=near(half, phase, step), device_id_type=MESH,
        ).start()

    def arrive(dst, stage, c):
        pltpu.make_async_copy(dst.at[c], dst.at[c], ring_recv.at[stage, c]).wait()

    def hop(at, step):
        return lax.rem(at + step + SIDE, SIDE)

    def stage1(c):
        for half in range(2):
            far = hop(first[half], 2)
            for step in (1, -1):
                send(part.at[c, half, far, pl.ds(1 - step, 2)], r1, 0, c, half, 0, step)

    def stage2(c):
        arrive(r1, 0, c)
        for half in range(2):
            for step in (1, -1):
                to = hop(first[half], step)
                at = pl.ds(1 - step, 2)
                part[c, half, to, at] = part[c, half, to, at] + r1[c, half, (1 - step) // 2]
                send(part.at[c, half, to], r2, 1, c, half, 0, step)

    def stage3(c):
        arrive(r2, 1, c)
        for half in range(2):
            me = first[half]
            part[c, half, me] = part[c, half, me] + r2[c, half, 0] + r2[c, half, 1]
            for step in range(1, SIDE):
                to = hop(second[half], step)
                pltpu.make_async_remote_copy(
                    part.at[c, half, me, to], r3.at[c, half, step - 1], ring_send.at[2], ring_recv.at[2, c],
                    device_id=near(half, 1, step), device_id_type=MESH,
                ).start()

    def stage4(c):
        arrive(r3, 2, c)
        for half in range(2):
            at = pl.ds(pl.multiple_of(c * HALF + half * 16, 16), 16)
            total = part[c, half, first[half], second[half]]
            for step in range(1, SIDE):
                total = total + r3[c, half, step - 1]
            pair[at] = total

    stages = (stage2, stage3, stage4)

    def fill(c):
        blocks = compute(c)
        for n in range(2):
            at = slice(8 * n, 8 * n + 8)
            part[c, 0, :, :, at] = blocks[n].reshape(SIDE, SIDE, 8, 128)
            square = blocks[2 + n].reshape(SIDE, SIDE, 8, 128)
            for k in range(SIDE):
                part[c, 1, :, k, at] = square[k]

    @pl.loop(0, EARLY)
    def _(c):
        fill(c)

    met(0)
    greet(1)

    @pl.loop(0, EARLY)
    def _(c):
        stage1(c)

    @pl.loop(EARLY, RING)
    def _(c):
        fill(c)
        stage1(c)
        for n in range(1, ROUNDS):
            @pl.when(c == EARLY + 2 * n - 1)
            def _(n=n):
                met(n)
                if n + 1 < ROUNDS:
                    greet(n + 1)

        for n, stage in enumerate(stages):
            @pl.when(c >= LAG * (n + 1))
            def _(n=n, stage=stage):
                stage(c - LAG * (n + 1))

    small[2].wait()
    basis = jnp.concatenate([start[:, :PACKED], start[:, PACKED:]], axis=0)

    @pl.loop(RING, RING + 3 * LAG)
    def _(c):
        for n, stage in enumerate(stages):
            at = c - LAG * (n + 1)

            @pl.when((at >= 0) & (at < RING))
            def _(at=at, stage=stage):
                stage(at)

    def sum_over_gx(n, rows, value):
        src = left_out.at[n, pl.ds(0, rows)]
        dst = left_in.at[n, :, pl.ds(0, rows)]
        src[...] = value

        @pl.loop(1, GX)
        def _(r):
            pltpu.make_async_remote_copy(
                src, left_in.at[n, r - 1, pl.ds(0, rows)], x_send.at[n], x_recv.at[n],
                device_id={"gx": lax.rem(mx + r, GX)}, device_id_type=MESH,
            ).start()

        pltpu.make_async_copy(dst, dst, x_recv.at[n]).wait()
        total = value
        for r in range(GX - 1):
            total = total + left_in[n, r, :rows]
        return total, lambda: pltpu.make_async_copy(dst, dst, x_send.at[n]).wait()

    def sum_over_gy(n, value, beside):
        image[n] = value

        @pl.loop(1, GY)
        def _(r):
            dest = lax.rem(my + r, GY)
            pltpu.make_async_remote_copy(
                image.at[n, pl.ds(pl.multiple_of(dest * SHARE, SHARE), SHARE)], share_in.at[n, r - 1],
                s_send.at[n], s_recv.at[n], device_id={"gy": dest}, device_id_type=MESH,
            ).start()

        pltpu.make_async_copy(share_in.at[n], share_in.at[n], s_recv.at[n]).wait()
        total = image[n, pl.ds(pl.multiple_of(my * SHARE, SHARE), SHARE)]
        for r in range(GY - 1):
            total = total + share_in[n, r]
        share[n] = total
        full[n, my] = total

        @pl.loop(1, GY)
        def _(r):
            pltpu.make_async_remote_copy(
                share.at[n], full.at[n, my], g_send.at[n], g_recv.at[n],
                device_id={"gy": lax.rem(my + r, GY)}, device_id_type=MESH,
            ).start()

        aside = beside()
        pltpu.make_async_copy(share_in.at[n], share_in.at[n], g_recv.at[n]).wait()

        def end():
            pltpu.make_async_copy(share_in.at[n], share_in.at[n], s_send.at[n]).wait()
            pltpu.make_async_copy(share_in.at[n], share_in.at[n], g_send.at[n]).wait()

        return full[n].reshape(128, PACKED), aside, end

    low64 = lower_lanes((64, 128))
    units = pair[...]
    total, end0 = sum_over_gx(0, 32, pair_up(fold(dot(basis, units))))
    image1, _, end1 = sum_over_gy(0, dot(twice(unpair(total)), units, NT), lambda: None)
    left = fold(dot(image1, units))
    gram = fold(dot(image1, image1, NT))
    total, end2 = sum_over_gx(1, 64, jnp.where(low64, left, swap(gram)))
    raw, factor, end3 = sum_over_gy(
        1, dot(twice(total), units, NT), lambda: inverse_factor(swap(total))
    )
    image2 = dot(twice(factor), raw)
    gram = fold(dot(image2, image2, NT))
    total, end4 = sum_over_gx(2, 32, pair_up(gram))
    factor = inverse_factor(unpair(total))
    final = dot(twice(factor), image2) * jnp.sqrt(F32(ROWS * GX))
    out_ref[:, :PACKED] = final[:64]
    out_ref[:, PACKED:] = final[64:]
    for n, ref in enumerate((r1, r2, r3)):
        pltpu.make_async_copy(ref, ref, ring_send.at[n]).wait()
    for end in (end0, end1, end2, end3, end4):
        end()


def on_device(field, mode2_factor, mode3_factor, start_factor):
    dma = pltpu.SemaphoreType.DMA
    out = pl.pallas_call(
        kernel,
        out_shape=jax.ShapeDtypeStruct((RANK, ROWS), F32),
        in_specs=[pl.BlockSpec(memory_space=pl.ANY)] * 4,
        out_specs=pl.BlockSpec(memory_space=pltpu.VMEM),
        scratch_shapes=[
            pltpu.VMEM((T3, ROWS, COLS), F32),
            pltpu.VMEM((RANK, COLS), F32),
            pltpu.VMEM((R3, T3), F32),
            pltpu.VMEM((RANK, ROWS), F32),
            pltpu.VMEM((RING, 2, SIDE, SIDE, 16, 128), F32),
            pltpu.VMEM((RING, 2, 2, 2, 16, 128), F32),
            pltpu.VMEM((RING, 2, 2, SIDE, 16, 128), F32),
            pltpu.VMEM((RING, 2, SIDE - 1, 16, 128), F32),
            pltpu.VMEM((PACKED, 128), F32),
            pltpu.VMEM((3, 64, 128), F32),
            pltpu.VMEM((3, GX - 1, 64, 128), F32),
            pltpu.VMEM((2, 128, PACKED), F32),
            pltpu.VMEM((2, GY - 1, SHARE, PACKED), F32),
            pltpu.VMEM((2, SHARE, PACKED), F32),
            pltpu.VMEM((2, GY, SHARE, PACKED), F32),
            dma((CHUNKS, 2)),
            dma((3,)),
            dma((3,)), dma((3, RING)),
            pltpu.SemaphoreType.REGULAR((ROUNDS - 1,)),
            dma((3,)), dma((3,)),
            dma((2,)), dma((2,)),
            dma((2,)), dma((2,)),
        ],
        compiler_params=pltpu.CompilerParams(
            collective_id=0, has_side_effects=True, vmem_limit_bytes=60 * 1024 * 1024
        ),
    )(field, mode2_factor.T, mode3_factor.T, start_factor.T)
    return out.T


def solution(mesh):
    placed = (P(None, "gx", "gy"), P("gy", None), P(), P("gx", None))
    return jax.shard_map(
        on_device, mesh=mesh, in_specs=placed, out_specs=P("gx", None), check_vma=False
    )
```

```python
import functools

import jax
import jax.numpy as jnp
from jax import lax
from jax.experimental import pallas as pl
from jax.experimental.pallas import tpu as pltpu
from jax.sharding import PartitionSpec as P

MESH = pl.DeviceIdType.MESH
HIGH = lax.Precision.HIGHEST
F32 = jnp.float32
BF16 = jnp.bfloat16

T3 = 32
R3 = 16
RANK = 64
ROWS = 512
COLS = 256
GX = 8
GY = 16
CHUNKS = 8
HALF = ROWS // CHUNKS // 2
RING = CHUNKS
LAG = 6
EARLY = 3
STEP = 8
SECOND = 5
THIRD = 11
SIDE = 4
PACKED = ROWS // 2
SHARE = 128 // GY
NN = (((1,), (0,)), ((), ()))
NT = (((1,), (1,)), ((), ()))


def dot(a, b, dims=NN):
    return lax.dot_general(a, b, dims, precision=HIGH, preferred_element_type=F32)


def bdot(a, b):
    return lax.dot_general(a, b, NN, preferred_element_type=F32)


def split(a):
    high = a.astype(BF16)
    return high, (a - high.astype(F32)).astype(BF16)


def swap(a):
    return pltpu.roll(a, 64, 1)


def lower_lanes(shape):
    return lax.broadcasted_iota(jnp.int32, shape, 1) < 64


def fold(m):
    return m[:64] + swap(m[64:])


def pair_up(s):
    return jnp.where(lower_lanes((32, 128)), s[:32], swap(s[32:]))


def unpair(p):
    return jnp.concatenate([p, swap(p)], axis=0)


def twice(s):
    low = lower_lanes((64, 128))
    zero = jnp.zeros_like(s)
    return jnp.concatenate([jnp.where(low, s, zero), jnp.where(low, zero, swap(s))], axis=0)


def inverse_factor(gram):
    lane = lax.broadcasted_iota(jnp.int32, (8, 128), 1)
    row = lax.broadcasted_iota(jnp.int32, (8, 128), 0)
    tiles = []
    for b in range(8):
        unit = jnp.where(lane == row + (64 + 8 * b), 1.0, 0.0)
        tiles.append(jnp.where(lane < 64, gram[8 * b : 8 * b + 8], unit))
    wide = lambda a: jnp.broadcast_to(a, (8, 128))
    for k in range(0, 64, STEP):
        own, at = divmod(k, 8)
        lines = [wide(tiles[own][at + j : at + j + 1]) for j in range(STEP)]
        cols = [[wide(t[:, k + j : k + j + 1]) for t in tiles[own:]] for j in range(STEP)]
        entry = [[wide(cols[j][0][at + n : at + n + 1]) if n >= j else None for n in range(STEP)] for j in range(STEP)]
        for j in range(STEP):
            inverse = 1.0 / entry[j][j]
            for n in range(j + 1, STEP):
                ratio = entry[j][n] * inverse
                for i in range(n, STEP):
                    entry[n][i] = entry[n][i] - ratio * entry[j][i]
                lines[n] = lines[n] - ratio * lines[j]
                cols[n] = [c - ratio * d for c, d in zip(cols[n], cols[j])]
            scaled = lines[j] * inverse
            for b in range(own, 8):
                col = cols[j][b - own]
                if b == own:
                    col = jnp.where(row > at + j, col, 0.0)
                tiles[b] = tiles[b] - col * scaled
    out = []
    for b in range(8):
        diag = jnp.sum(jnp.where(lane == row + 8 * b, tiles[b], 0.0), axis=1, keepdims=True)
        out.append(tiles[b] * lax.rsqrt(diag))
    return swap(jnp.concatenate(out, axis=0))


def kernel(
    field_hbm, m2_hbm, m3_hbm, start_hbm, out_ref,
    field, m2, m3, start,
    part, r1, r2, r3, pair, left_out, left_in, image, share_in, share, full, basis, lead, lead_in, lead_gx, lead_gy, lead_all,
    lead_send, lead_recv, in_sem, small_sem, ring_send, ring_recv, x_send, x_recv, s_send, s_recv, g_send, g_recv,
):
    mx = lax.axis_index("gx")
    my = lax.axis_index("gy")

    small = [
        pltpu.make_async_copy(src, dst, small_sem.at[n])
        for n, (src, dst) in enumerate(((m2_hbm, m2), (m3_hbm, m3), (start_hbm, start)))
    ]
    def load(c, h):
        at = pl.ds(pl.multiple_of(h * PACKED + c * HALF, HALF), HALF)
        return pltpu.make_async_copy(field_hbm.at[:, at, :], field.at[:, at, :], in_sem.at[c, h])

    small[0].start()
    small[1].start()
    for c in range(CHUNKS):
        for h in range(2):
            load(c, h).start()
    small[2].start()

    px, py = my // SIDE, lax.rem(my, SIDE)
    barrier = pltpu.get_barrier_semaphore()

    @pl.loop(1, GY)
    def _(r):
        pl.semaphore_signal(barrier, inc=1, device_id={"gy": lax.rem(my + r, GY)}, device_id_type=MESH)

    @pl.loop(1, GX)
    def _(r):
        pl.semaphore_signal(barrier, inc=1, device_id={"gx": lax.rem(mx + r, GX)}, device_id_type=MESH)

    small[0].wait()
    small[1].wait()
    m2h, m2l = split(jnp.transpose(m2[...]))
    right = jnp.concatenate([m2h, m2l], axis=1)
    tall = jnp.where(
        lax.broadcasted_iota(jnp.int32, (128, R3), 0) // 8 == lax.broadcasted_iota(jnp.int32, (128, R3), 1), 1.0, 0.0
    )
    wide = jnp.where(
        lax.broadcasted_iota(jnp.int32, (T3, 256), 0) == lax.broadcasted_iota(jnp.int32, (T3, 256), 1) // 8, 1.0, 0.0
    )
    spread = dot(dot(tall, m3[...]), wide)
    same = (
        lax.broadcasted_iota(jnp.int32, (128, 256), 0) % 8 == lax.broadcasted_iota(jnp.int32, (128, 256), 1) % 8
    )
    wh, wl = split(jnp.where(same, spread, 0.0))
    w2 = jnp.concatenate([wh, wl], axis=0)
    low = lower_lanes((256, 128))
    low64 = lower_lanes((64, 128))

    def project(i0):
        tile = field[:, pl.ds(i0, 8), :].reshape(T3 * 8, COLS)
        th, tl = split(tile)
        return bdot(th, right) + bdot(tl, right)

    def compute(c):
        pairs = []
        for h in range(2):
            load(c, h).wait()
        for n in range(HALF // 8):
            i0 = pl.multiple_of(c * HALF + n * 8, 8)
            a, b = project(i0), project(i0 + PACKED)
            pairs.append(jnp.where(low, a + swap(a), b + swap(b)))
        blocks = []
        for n in range(0, HALF // 8, 2):
            bh, bl = split(jnp.concatenate(pairs[n : n + 2], axis=1))
            two = bdot(w2, bh)
            res = two[:128] + two[128:] + bdot(wh, bl)
            blocks += [res[:, :128].reshape(R3, 8, 128), res[:, 128:].reshape(R3, 8, 128)]
        return blocks

    first, second = (px, py), (py, px)

    def near(half, phase, step):
        if (half + phase) % 2 == 0:
            return {"gy": lax.rem(px + step + SIDE, SIDE) * SIDE + py}
        return {"gy": px * SIDE + lax.rem(py + step + SIDE, SIDE)}

    def send(src, dst, stage, c, half, phase, step):
        pltpu.make_async_remote_copy(
            src, dst.at[c, half, (1 - step) // 2], ring_send.at[stage], ring_recv.at[stage, c],
            device_id=near(half, phase, step), device_id_type=MESH,
        ).start()

    def arrive(dst, stage, c):
        pltpu.make_async_copy(dst.at[c], dst.at[c], ring_recv.at[stage, c]).wait()

    def hop(at, step):
        return lax.rem(at + step + SIDE, SIDE)

    def stage1(c):
        for half in range(2):
            far = hop(first[half], 2)
            for step in (1, -1):
                send(part.at[c, half, far, pl.ds(1 - step, 2)], r1, 0, c, half, 0, step)

    def stage2(c):
        arrive(r1, 0, c)
        for half in range(2):
            for step in (1, -1):
                to = hop(first[half], step)
                at = pl.ds(1 - step, 2)
                part[c, half, to, at] = part[c, half, to, at] + r1[c, half, (1 - step) // 2]
                send(part.at[c, half, to], r2, 1, c, half, 0, step)

    def stage3(c):
        arrive(r2, 1, c)
        for half in range(2):
            me = first[half]
            part[c, half, me] = part[c, half, me] + r2[c, half, 0] + r2[c, half, 1]
            for step in range(1, SIDE):
                to = hop(second[half], step)
                pltpu.make_async_remote_copy(
                    part.at[c, half, me, to], r3.at[c, half, step - 1], ring_send.at[2], ring_recv.at[2, c],
                    device_id=near(half, 1, step), device_id_type=MESH,
                ).start()

    def stage4(c):
        arrive(r3, 2, c)
        for half in range(2):
            at = pl.ds(pl.multiple_of(c * HALF + half * 16, 16), 16)
            total = part[c, half, first[half], second[half]]
            for step in range(1, SIDE):
                total = total + r3[c, half, step - 1]
            pair[at] = total

    stages = (stage2, stage3, stage4)

    def fill(c):
        blocks = compute(c)
        for n in range(2):
            at = slice(8 * n, 8 * n + 8)
            part[c, 0, :, :, at] = blocks[n].reshape(SIDE, SIDE, 8, 128)
            square = blocks[2 + n].reshape(SIDE, SIDE, 8, 128)
            for k in range(SIDE):
                part[c, 1, :, k, at] = square[k]

    small[2].wait()
    for h in range(2):
        for n, piece in enumerate(split(start[:, h * PACKED : h * PACKED + PACKED])):
            basis[n, 64 * h : 64 * h + 64] = piece

    def lead_part(k):
        at = pl.ds(pl.multiple_of(k * 128, 128), 128)
        bh, bl = basis[0, :, at], basis[1, :, at]
        both = jnp.concatenate([bh, bl], axis=0)

        def rows(x, y):
            halves = [part[pl.ds(4 * k, 4), 0, x, y], part[pl.ds(4 * k, 4), 1, y, x]]
            return jnp.stack(halves, axis=1).reshape(128, 128)

        for s in range(R3 // 2):
            x, y = divmod(s, SIDE)
            uh, ul = split(jnp.concatenate([rows(x, y), rows(x + 2, y)], axis=1))
            two = bdot(both, uh)
            m = two[:128] + two[128:] + bdot(bh, ul)
            value = jnp.where(low64, m[:64, :128] + swap(m[64:, :128]), m[64:, 128:] + swap(m[:64, 128:]))
            value = value.reshape(8, 8, 128)
            lead[:, s] = jnp.where(k == 0, value, lead[:, s] + value)

    def lead_stage1():
        @pl.loop(1, GX)
        def _(r):
            dest = lax.rem(mx + r, GX)
            pltpu.make_async_remote_copy(
                lead.at[dest], lead_in.at[r - 1], lead_send.at[0], lead_recv.at[0],
                device_id={"gx": dest}, device_id_type=MESH,
            ).start()

    def lead_stage2():
        pltpu.make_async_copy(lead_in, lead_in, lead_recv.at[0]).wait()
        total = lead[mx]
        for r in range(GX - 1):
            total = total + lead_in[r]
        lead_gx[...] = total

        @pl.loop(1, GY)
        def _(r):
            dest = lax.rem(my + r, GY)
            pltpu.make_async_remote_copy(
                lead_gx.at[lax.rem(dest, 8)], lead_gy.at[r - 1], lead_send.at[1], lead_recv.at[1],
                device_id={"gy": dest}, device_id_type=MESH,
            ).start()

    def lead_stage3():
        pltpu.make_async_copy(lead_gy, lead_gy, lead_recv.at[1]).wait()
        total = lead_gx[lax.rem(my, 8)]
        for r in range(GY - 1):
            total = total + lead_gy[r]
        lead_all[mx] = jnp.where(my < 8, total, swap(total))

        @pl.loop(1, GX)
        def _(r):
            pltpu.make_async_remote_copy(
                lead_all.at[mx], lead_all.at[mx], lead_send.at[2], lead_recv.at[2],
                device_id={"gx": lax.rem(mx + r, GX)}, device_id_type=MESH,
            ).start()

    @pl.loop(0, EARLY)
    def _(c):
        fill(c)

    pl.semaphore_wait(barrier, GX + GY - 2)

    @pl.loop(0, EARLY)
    def _(c):
        stage1(c)

    @pl.loop(EARLY, RING)
    def _(c):
        fill(c)
        stage1(c)

        @pl.when(lax.rem(c, 4) == 3)
        def _():
            lead_part(c // 4)

        for n, stage in enumerate(stages):
            @pl.when(c >= LAG * (n + 1))
            def _(n=n, stage=stage):
                stage(c - LAG * (n + 1))

    lead_stage1()

    @pl.loop(RING, RING + 3 * LAG)
    def _(c):
        @pl.when(c == RING + SECOND)
        def _():
            lead_stage2()

        @pl.when(c == RING + THIRD)
        def _():
            lead_stage3()

        for n, stage in enumerate(stages):
            at = c - LAG * (n + 1)

            @pl.when((at >= 0) & (at < RING))
            def _(at=at, stage=stage):
                stage(at)

    def sum_over_gx(n, value):
        left_out[n] = value

        @pl.loop(1, GX)
        def _(r):
            pltpu.make_async_remote_copy(
                left_out.at[n], left_in.at[n, r - 1], x_send.at[n], x_recv.at[n],
                device_id={"gx": lax.rem(mx + r, GX)}, device_id_type=MESH,
            ).start()

        def finish():
            pltpu.make_async_copy(left_in.at[n], left_in.at[n], x_recv.at[n]).wait()
            total = value
            for r in range(GX - 1):
                total = total + left_in[n, r]
            return unpair(total)

        return finish, lambda: pltpu.make_async_copy(left_in.at[n], left_in.at[n], x_send.at[n]).wait()

    def sum_over_gy(n, value, beside):
        image[n] = value

        @pl.loop(1, GY)
        def _(r):
            dest = lax.rem(my + r, GY)
            pltpu.make_async_remote_copy(
                image.at[n, pl.ds(pl.multiple_of(dest * SHARE, SHARE), SHARE)], share_in.at[n, r - 1],
                s_send.at[n], s_recv.at[n], device_id={"gy": dest}, device_id_type=MESH,
            ).start()

        pltpu.make_async_copy(share_in.at[n], share_in.at[n], s_recv.at[n]).wait()
        total = image[n, pl.ds(pl.multiple_of(my * SHARE, SHARE), SHARE)]
        for r in range(GY - 1):
            total = total + share_in[n, r]
        share[n] = total
        full[n, my] = total

        @pl.loop(1, GY)
        def _(r):
            pltpu.make_async_remote_copy(
                share.at[n], full.at[n, my], g_send.at[n], g_recv.at[n],
                device_id={"gy": lax.rem(my + r, GY)}, device_id_type=MESH,
            ).start()

        aside = beside()
        pltpu.make_async_copy(share_in.at[n], share_in.at[n], g_recv.at[n]).wait()

        def end():
            pltpu.make_async_copy(share_in.at[n], share_in.at[n], s_send.at[n]).wait()
            pltpu.make_async_copy(share_in.at[n], share_in.at[n], g_send.at[n]).wait()

        return full[n].reshape(128, PACKED), aside, end

    uh, ul = split(pair[...])

    def times_units(a, dims):
        ah, al = split(a)
        three = functools.partial(lax.dot_general, dimension_numbers=dims, preferred_element_type=F32)
        two = three(jnp.concatenate([ah, al], axis=0), uh)
        return two[:128] + two[128:] + three(ah, ul)

    pltpu.make_async_copy(lead_all.at[pl.ds(0, 7)], lead_all.at[pl.ds(0, 7)], lead_recv.at[2]).wait()
    image1, _, end1 = sum_over_gy(0, times_units(twice(lead_all[...].reshape(64, 128)), NT), lambda: None)
    finish_left, end2 = sum_over_gx(0, pair_up(fold(times_units(image1, NN))))
    finish_gram, end5 = sum_over_gx(2, pair_up(fold(dot(image1, image1, NT))))
    raw, factor, end3 = sum_over_gy(
        1, times_units(twice(finish_left()), NT), lambda: inverse_factor(finish_gram())
    )
    image2 = dot(twice(factor), raw)
    finish_gram, end4 = sum_over_gx(1, pair_up(fold(dot(image2, image2, NT))))
    factor = inverse_factor(finish_gram())
    final = dot(twice(factor), image2) * jnp.sqrt(F32(ROWS * GX))
    out_ref[:, :PACKED] = final[:64]
    out_ref[:, PACKED:] = final[64:]
    for n, ref in enumerate((r1, r2, r3)):
        pltpu.make_async_copy(ref, ref, ring_send.at[n]).wait()
    for n, ref in enumerate((lead_in, lead_gy, lead_all.at[pl.ds(0, 7)])):
        pltpu.make_async_copy(ref, ref, lead_send.at[n]).wait()
    for end in (end1, end2, end3, end4, end5):
        end()


def on_device(field, mode2_factor, mode3_factor, start_factor):
    dma = pltpu.SemaphoreType.DMA
    out = pl.pallas_call(
        kernel,
        out_shape=jax.ShapeDtypeStruct((RANK, ROWS), F32),
        in_specs=[pl.BlockSpec(memory_space=pl.ANY)] * 4,
        out_specs=pl.BlockSpec(memory_space=pltpu.VMEM),
        scratch_shapes=[
            pltpu.VMEM((T3, ROWS, COLS), F32),
            pltpu.VMEM((RANK, COLS), F32),
            pltpu.VMEM((R3, T3), F32),
            pltpu.VMEM((RANK, ROWS), F32),
            pltpu.VMEM((RING, 2, SIDE, SIDE, 16, 128), F32),
            pltpu.VMEM((RING, 2, 2, 2, 16, 128), F32),
            pltpu.VMEM((RING, 2, 2, SIDE, 16, 128), F32),
            pltpu.VMEM((RING, 2, SIDE - 1, 16, 128), F32),
            pltpu.VMEM((PACKED, 128), F32),
            pltpu.VMEM((3, 32, 128), F32),
            pltpu.VMEM((3, GX - 1, 32, 128), F32),
            pltpu.VMEM((2, 128, PACKED), F32),
            pltpu.VMEM((2, GY - 1, SHARE, PACKED), F32),
            pltpu.VMEM((2, SHARE, PACKED), F32),
            pltpu.VMEM((2, GY, SHARE, PACKED), F32),
            pltpu.VMEM((2, 128, PACKED), BF16),
            pltpu.VMEM((GX, 8, 8, 128), F32),
            pltpu.VMEM((GX - 1, 8, 8, 128), F32),
            pltpu.VMEM((8, 8, 128), F32),
            pltpu.VMEM((GY - 1, 8, 128), F32),
            pltpu.VMEM((GX, 8, 128), F32),
            dma((3,)), dma((3,)),
            dma((CHUNKS, 2)),
            dma((3,)),
            dma((3,)), dma((3, RING)),
            dma((3,)), dma((3,)),
            dma((2,)), dma((2,)),
            dma((2,)), dma((2,)),
        ],
        compiler_params=pltpu.CompilerParams(
            collective_id=0, has_side_effects=True, vmem_limit_bytes=60 * 1024 * 1024
        ),
    )(field, mode2_factor.T, mode3_factor.T, start_factor.T)
    return out.T


def solution(mesh):
    placed = (P(None, "gx", "gy"), P("gy", None), P(), P("gx", None))
    return jax.shard_map(
        on_device, mesh=mesh, in_specs=placed, out_specs=P("gx", None), check_vma=False
    )
```

```python
import functools

import jax
import jax.numpy as jnp
from jax import lax
from jax.experimental import pallas as pl
from jax.experimental.pallas import tpu as pltpu
from jax.sharding import PartitionSpec as P

MESH = pl.DeviceIdType.MESH
HIGH = lax.Precision.HIGHEST
F32 = jnp.float32
BF16 = jnp.bfloat16

T3 = 32
R3 = 16
RANK = 64
ROWS = 512
COLS = 256
GX = 8
GY = 16
CHUNKS = 8
HALF = ROWS // CHUNKS // 2
RING = CHUNKS
LAG = 8
EARLY = 3
STEP = 8
SECOND = 6
THIRD = 14
SIDE = 4
PACKED = ROWS // 2
SHARE = 128 // GY
NN = (((1,), (0,)), ((), ()))
NT = (((1,), (1,)), ((), ()))


def dot(a, b, dims=NN):
    return lax.dot_general(a, b, dims, precision=HIGH, preferred_element_type=F32)


def bdot(a, b):
    return lax.dot_general(a, b, NN, preferred_element_type=F32)


def split(a):
    high = a.astype(BF16)
    return high, (a - high.astype(F32)).astype(BF16)


def swap(a):
    return pltpu.roll(a, 64, 1)


def lower_lanes(shape):
    return lax.broadcasted_iota(jnp.int32, shape, 1) < 64


def fold(m):
    return m[:64] + swap(m[64:])


def pair_up(s):
    return jnp.where(lower_lanes((32, 128)), s[:32], swap(s[32:]))


def unpair(p):
    return jnp.concatenate([p, swap(p)], axis=0)


def twice(s):
    low = lower_lanes((64, 128))
    zero = jnp.zeros_like(s)
    return jnp.concatenate([jnp.where(low, s, zero), jnp.where(low, zero, swap(s))], axis=0)


def inverse_factor(gram):
    lane = lax.broadcasted_iota(jnp.int32, (8, 128), 1)
    row = lax.broadcasted_iota(jnp.int32, (8, 128), 0)
    tiles = []
    for b in range(8):
        unit = jnp.where(lane == row + (64 + 8 * b), 1.0, 0.0)
        tiles.append(jnp.where(lane < 64, gram[8 * b : 8 * b + 8], unit))
    wide = lambda a: jnp.broadcast_to(a, (8, 128))
    for k in range(0, 64, STEP):
        own, at = divmod(k, 8)
        lines = [wide(tiles[own][at + j : at + j + 1]) for j in range(STEP)]
        cols = [[wide(t[:, k + j : k + j + 1]) for t in tiles[own:]] for j in range(STEP)]
        entry = [[wide(cols[j][0][at + n : at + n + 1]) if n >= j else None for n in range(STEP)] for j in range(STEP)]
        for j in range(STEP):
            inverse = 1.0 / entry[j][j]
            for n in range(j + 1, STEP):
                ratio = entry[j][n] * inverse
                for i in range(n, STEP):
                    entry[n][i] = entry[n][i] - ratio * entry[j][i]
                lines[n] = lines[n] - ratio * lines[j]
                cols[n] = [c - ratio * d for c, d in zip(cols[n], cols[j])]
            scaled = lines[j] * inverse
            for b in range(own, 8):
                col = cols[j][b - own]
                if b == own:
                    col = jnp.where(row > at + j, col, 0.0)
                tiles[b] = tiles[b] - col * scaled
    out = []
    for b in range(8):
        diag = jnp.sum(jnp.where(lane == row + 8 * b, tiles[b], 0.0), axis=1, keepdims=True)
        out.append(tiles[b] * lax.rsqrt(diag))
    return swap(jnp.concatenate(out, axis=0))


def kernel(
    field_hbm, m2_hbm, m3_hbm, start_hbm, out_ref,
    field, m2, m3, start,
    part, r1, r2, r3, pair, left_out, left_in, image, share_in, share, full, basis, lead, lead_in, lead_gx, lead_gy, lead_all,
    lead_send, lead_recv, in_sem, small_sem, ring_send, ring_recv, x_send, x_recv, s_send, s_recv, g_send, g_recv,
):
    mx = lax.axis_index("gx")
    my = lax.axis_index("gy")

    small = [
        pltpu.make_async_copy(src, dst, small_sem.at[n])
        for n, (src, dst) in enumerate(((m2_hbm, m2), (m3_hbm, m3), (start_hbm, start)))
    ]
    def load(c, h):
        at = pl.ds(pl.multiple_of(h * PACKED + c * HALF, HALF), HALF)
        return pltpu.make_async_copy(field_hbm.at[:, at, :], field.at[:, at, :], in_sem.at[c, h])

    small[0].start()
    small[1].start()
    for c in range(CHUNKS):
        for h in range(2):
            load(c, h).start()
    small[2].start()

    px, py = my // SIDE, lax.rem(my, SIDE)
    barrier = pltpu.get_barrier_semaphore()

    @pl.loop(1, GY)
    def _(r):
        pl.semaphore_signal(barrier, inc=1, device_id={"gy": lax.rem(my + r, GY)}, device_id_type=MESH)

    @pl.loop(1, GX)
    def _(r):
        pl.semaphore_signal(barrier, inc=1, device_id={"gx": lax.rem(mx + r, GX)}, device_id_type=MESH)

    small[0].wait()
    small[1].wait()
    m2h, m2l = split(jnp.transpose(m2[...]))
    right = jnp.concatenate([m2h, m2l], axis=1)
    tall = jnp.where(
        lax.broadcasted_iota(jnp.int32, (128, R3), 0) // 8 == lax.broadcasted_iota(jnp.int32, (128, R3), 1), 1.0, 0.0
    )
    wide = jnp.where(
        lax.broadcasted_iota(jnp.int32, (T3, 256), 0) == lax.broadcasted_iota(jnp.int32, (T3, 256), 1) // 8, 1.0, 0.0
    )
    same = (
        lax.broadcasted_iota(jnp.int32, (128, 256), 0) % 8 == lax.broadcasted_iota(jnp.int32, (128, 256), 1) % 8
    )
    wh, wl = (
        jnp.where(same, bdot(bdot(tall.astype(BF16), piece).astype(BF16), wide.astype(BF16)), 0.0).astype(BF16)
        for piece in split(m3[...])
    )
    w2 = jnp.concatenate([wh, wl], axis=0)
    low = lower_lanes((256, 128))
    low64 = lower_lanes((64, 128))

    def project(i0):
        tile = field[:, pl.ds(i0, 8), :].reshape(T3 * 8, COLS)
        th, tl = split(tile)
        return bdot(th, right) + bdot(tl, right)

    def compute(c):
        pairs = []
        for h in range(2):
            load(c, h).wait()
        for n in range(HALF // 8):
            i0 = pl.multiple_of(c * HALF + n * 8, 8)
            a, b = project(i0), project(i0 + PACKED)
            pairs.append(jnp.where(low, a + swap(a), b + swap(b)))
        blocks = []
        for n in range(0, HALF // 8, 2):
            bh, bl = split(jnp.concatenate(pairs[n : n + 2], axis=1))
            two = bdot(w2, bh)
            res = two[:128] + two[128:] + bdot(wh, bl)
            blocks += [res[:, :128].reshape(R3, 8, 128), res[:, 128:].reshape(R3, 8, 128)]
        return blocks

    first, second = (px, py), (py, px)

    def near(half, phase, step):
        if (half + phase) % 2 == 0:
            return {"gy": lax.rem(px + step + SIDE, SIDE) * SIDE + py}
        return {"gy": px * SIDE + lax.rem(py + step + SIDE, SIDE)}

    def send(src, dst, stage, c, half, phase, step):
        pltpu.make_async_remote_copy(
            src, dst.at[c, half, (1 - step) // 2], ring_send.at[stage], ring_recv.at[stage, c],
            device_id=near(half, phase, step), device_id_type=MESH,
        ).start()

    def arrive(dst, stage, c):
        pltpu.make_async_copy(dst.at[c], dst.at[c], ring_recv.at[stage, c]).wait()

    def hop(at, step):
        return lax.rem(at + step + SIDE, SIDE)

    def stage1(c):
        for half in range(2):
            far = hop(first[half], 2)
            for step in (1, -1):
                send(part.at[c, half, far, pl.ds(1 - step, 2)], r1, 0, c, half, 0, step)

    def stage2(c):
        arrive(r1, 0, c)
        for half in range(2):
            for step in (1, -1):
                to = hop(first[half], step)
                at = pl.ds(1 - step, 2)
                part[c, half, to, at] = part[c, half, to, at] + r1[c, half, (1 - step) // 2]
                send(part.at[c, half, to], r2, 1, c, half, 0, step)

    def stage3(c):
        arrive(r2, 1, c)
        for half in range(2):
            me = first[half]
            part[c, half, me] = part[c, half, me] + r2[c, half, 0] + r2[c, half, 1]
            for step in range(1, SIDE):
                to = hop(second[half], step)
                pltpu.make_async_remote_copy(
                    part.at[c, half, me, to], r3.at[c, half, step - 1], ring_send.at[2], ring_recv.at[2, c],
                    device_id=near(half, 1, step), device_id_type=MESH,
                ).start()

    def stage4(c):
        arrive(r3, 2, c)
        for half in range(2):
            at = pl.ds(pl.multiple_of(c * HALF + half * 16, 16), 16)
            total = part[c, half, first[half], second[half]]
            for step in range(1, SIDE):
                total = total + r3[c, half, step - 1]
            pair[at] = total

    stages = (stage2, stage3, stage4)

    def fill(c):
        blocks = compute(c)
        for n in range(2):
            at = slice(8 * n, 8 * n + 8)
            part[c, 0, :, :, at] = blocks[n].reshape(SIDE, SIDE, 8, 128)
            square = blocks[2 + n].reshape(SIDE, SIDE, 8, 128)
            for k in range(SIDE):
                part[c, 1, :, k, at] = square[k]

    def lead_part():
        bh, bl = basis[0], basis[1]
        both = jnp.concatenate([bh, bl], axis=0)

        def rows(x, y):
            return jnp.stack([part[:, 0, x, y], part[:, 1, y, x]], axis=1).reshape(PACKED, 128)

        for s in range(R3 // 2):
            x, y = divmod(s, SIDE)
            uh, ul = split(jnp.concatenate([rows(x, y), rows(x + 2, y)], axis=1))
            two = bdot(both, uh)
            m = two[:128] + two[128:] + bdot(bh, ul)
            value = jnp.where(low64, m[:64, :128] + swap(m[64:, :128]), m[64:, 128:] + swap(m[:64, 128:]))
            value = value.reshape(8, 8, 128)
            lead[:, s] = value

    def lead_stage1():
        @pl.loop(1, GX)
        def _(r):
            dest = lax.rem(mx + r, GX)
            pltpu.make_async_remote_copy(
                lead.at[dest], lead_in.at[r - 1], lead_send.at[0], lead_recv.at[0],
                device_id={"gx": dest}, device_id_type=MESH,
            ).start()

    def lead_stage2():
        pltpu.make_async_copy(lead_in, lead_in, lead_recv.at[0]).wait()
        total = lead[mx]
        for r in range(GX - 1):
            total = total + lead_in[r]
        lead_gx[...] = total

        @pl.loop(1, GY)
        def _(r):
            dest = lax.rem(my + r, GY)
            pltpu.make_async_remote_copy(
                lead_gx.at[lax.rem(dest, 8)], lead_gy.at[r - 1], lead_send.at[1], lead_recv.at[1],
                device_id={"gy": dest}, device_id_type=MESH,
            ).start()

    def lead_stage3():
        pltpu.make_async_copy(lead_gy, lead_gy, lead_recv.at[1]).wait()
        total = lead_gx[lax.rem(my, 8)]
        for r in range(GY - 1):
            total = total + lead_gy[r]
        lead_all[mx] = jnp.where(my < 8, total, swap(total))

        @pl.loop(1, GX)
        def _(r):
            pltpu.make_async_remote_copy(
                lead_all.at[mx], lead_all.at[mx], lead_send.at[2], lead_recv.at[2],
                device_id={"gx": lax.rem(mx + r, GX)}, device_id_type=MESH,
            ).start()

    @pl.loop(0, EARLY)
    def _(c):
        fill(c)

    small[2].wait()
    for h in range(2):
        for n, piece in enumerate(split(start[:, h * PACKED : h * PACKED + PACKED])):
            basis[n, 64 * h : 64 * h + 64] = piece

    pl.semaphore_wait(barrier, GX + GY - 2)

    @pl.loop(0, EARLY)
    def _(c):
        stage1(c)

    @pl.loop(EARLY, RING)
    def _(c):
        fill(c)
        stage1(c)

        for n, stage in enumerate(stages):
            @pl.when(c >= LAG * (n + 1))
            def _(n=n, stage=stage):
                stage(c - LAG * (n + 1))

    lead_part()
    lead_stage1()

    @pl.loop(RING, RING + 3 * LAG)
    def _(c):
        @pl.when(c == RING + SECOND)
        def _():
            lead_stage2()

        @pl.when(c == RING + THIRD)
        def _():
            lead_stage3()

        for n, stage in enumerate(stages):
            at = c - LAG * (n + 1)

            @pl.when((at >= 0) & (at < RING))
            def _(at=at, stage=stage):
                stage(at)

    def sum_over_gx(n, value):
        left_out[n] = value

        @pl.loop(1, GX)
        def _(r):
            pltpu.make_async_remote_copy(
                left_out.at[n], left_in.at[n, r - 1], x_send.at[n], x_recv.at[n],
                device_id={"gx": lax.rem(mx + r, GX)}, device_id_type=MESH,
            ).start()

        def finish():
            pltpu.make_async_copy(left_in.at[n], left_in.at[n], x_recv.at[n]).wait()
            total = value
            for r in range(GX - 1):
                total = total + left_in[n, r]
            return unpair(total)

        return finish, lambda: pltpu.make_async_copy(left_in.at[n], left_in.at[n], x_send.at[n]).wait()

    def sum_over_gy(n, value, beside):
        image[n] = value

        @pl.loop(1, GY)
        def _(r):
            dest = lax.rem(my + r, GY)
            pltpu.make_async_remote_copy(
                image.at[n, pl.ds(pl.multiple_of(dest * SHARE, SHARE), SHARE)], share_in.at[n, r - 1],
                s_send.at[n], s_recv.at[n], device_id={"gy": dest}, device_id_type=MESH,
            ).start()

        pltpu.make_async_copy(share_in.at[n], share_in.at[n], s_recv.at[n]).wait()
        total = image[n, pl.ds(pl.multiple_of(my * SHARE, SHARE), SHARE)]
        for r in range(GY - 1):
            total = total + share_in[n, r]
        share[n] = total
        full[n, my] = total

        @pl.loop(1, GY)
        def _(r):
            pltpu.make_async_remote_copy(
                share.at[n], full.at[n, my], g_send.at[n], g_recv.at[n],
                device_id={"gy": lax.rem(my + r, GY)}, device_id_type=MESH,
            ).start()

        aside = beside()
        pltpu.make_async_copy(share_in.at[n], share_in.at[n], g_recv.at[n]).wait()

        def end():
            pltpu.make_async_copy(share_in.at[n], share_in.at[n], s_send.at[n]).wait()
            pltpu.make_async_copy(share_in.at[n], share_in.at[n], g_send.at[n]).wait()

        return full[n].reshape(128, PACKED), aside, end

    uh, ul = split(pair[...])

    def times_units(a, dims):
        ah, al = split(a)
        three = functools.partial(lax.dot_general, dimension_numbers=dims, preferred_element_type=F32)
        two = three(jnp.concatenate([ah, al], axis=0), uh)
        return two[:128] + two[128:] + three(ah, ul)

    pltpu.make_async_copy(lead_all.at[pl.ds(0, 7)], lead_all.at[pl.ds(0, 7)], lead_recv.at[2]).wait()
    image1, _, end1 = sum_over_gy(0, times_units(twice(lead_all[...].reshape(64, 128)), NT), lambda: None)
    finish_left, end2 = sum_over_gx(0, pair_up(fold(times_units(image1, NN))))
    finish_gram, end5 = sum_over_gx(2, pair_up(fold(dot(image1, image1, NT))))
    raw, factor, end3 = sum_over_gy(
        1, times_units(twice(finish_left()), NT), lambda: inverse_factor(finish_gram())
    )
    image2 = dot(twice(factor), raw)
    finish_gram, end4 = sum_over_gx(1, pair_up(fold(dot(image2, image2, NT))))
    factor = inverse_factor(finish_gram())
    final = dot(twice(factor), image2) * jnp.sqrt(F32(ROWS * GX))
    out_ref[:, :PACKED] = final[:64]
    out_ref[:, PACKED:] = final[64:]
    for n, ref in enumerate((r1, r2, r3)):
        pltpu.make_async_copy(ref, ref, ring_send.at[n]).wait()
    for n, ref in enumerate((lead_in, lead_gy, lead_all.at[pl.ds(0, 7)])):
        pltpu.make_async_copy(ref, ref, lead_send.at[n]).wait()
    for end in (end1, end2, end3, end4, end5):
        end()


def on_device(field, mode2_factor, mode3_factor, start_factor):
    dma = pltpu.SemaphoreType.DMA
    out = pl.pallas_call(
        kernel,
        out_shape=jax.ShapeDtypeStruct((RANK, ROWS), F32),
        in_specs=[pl.BlockSpec(memory_space=pl.ANY)] * 4,
        out_specs=pl.BlockSpec(memory_space=pltpu.VMEM),
        scratch_shapes=[
            pltpu.VMEM((T3, ROWS, COLS), F32),
            pltpu.VMEM((RANK, COLS), F32),
            pltpu.VMEM((R3, T3), F32),
            pltpu.VMEM((RANK, ROWS), F32),
            pltpu.VMEM((RING, 2, SIDE, SIDE, 16, 128), F32),
            pltpu.VMEM((RING, 2, 2, 2, 16, 128), F32),
            pltpu.VMEM((RING, 2, 2, SIDE, 16, 128), F32),
            pltpu.VMEM((RING, 2, SIDE - 1, 16, 128), F32),
            pltpu.VMEM((PACKED, 128), F32),
            pltpu.VMEM((3, 32, 128), F32),
            pltpu.VMEM((3, GX - 1, 32, 128), F32),
            pltpu.VMEM((2, 128, PACKED), F32),
            pltpu.VMEM((2, GY - 1, SHARE, PACKED), F32),
            pltpu.VMEM((2, SHARE, PACKED), F32),
            pltpu.VMEM((2, GY, SHARE, PACKED), F32),
            pltpu.VMEM((2, 128, PACKED), BF16),
            pltpu.VMEM((GX, 8, 8, 128), F32),
            pltpu.VMEM((GX - 1, 8, 8, 128), F32),
            pltpu.VMEM((8, 8, 128), F32),
            pltpu.VMEM((GY - 1, 8, 128), F32),
            pltpu.VMEM((GX, 8, 128), F32),
            dma((3,)), dma((3,)),
            dma((CHUNKS, 2)),
            dma((3,)),
            dma((3,)), dma((3, RING)),
            dma((3,)), dma((3,)),
            dma((2,)), dma((2,)),
            dma((2,)), dma((2,)),
        ],
        compiler_params=pltpu.CompilerParams(
            collective_id=0, has_side_effects=True, vmem_limit_bytes=60 * 1024 * 1024
        ),
    )(field, mode2_factor.T, mode3_factor.T, start_factor.T)
    return out.T


def solution(mesh):
    placed = (P(None, "gx", "gy"), P("gy", None), P(), P("gx", None))
    return jax.shard_map(
        on_device, mesh=mesh, in_specs=placed, out_specs=P("gx", None), check_vma=False
    )
```

```python
import functools

import jax
import jax.numpy as jnp
from jax import lax
from jax.experimental import pallas as pl
from jax.experimental.pallas import tpu as pltpu
from jax.sharding import PartitionSpec as P

MESH = pl.DeviceIdType.MESH
HIGH = lax.Precision.HIGHEST
F32 = jnp.float32
BF16 = jnp.bfloat16

T3 = 32
R3 = 16
RANK = 64
ROWS = 512
COLS = 256
GX = 8
GY = 16
CHUNKS = 8
HALF = ROWS // CHUNKS // 2
RING = CHUNKS
LAG = 8
EARLY = 3
STEP = 8
SECOND = 6
THIRD = 14
SIDE = 4
PACKED = ROWS // 2
SHARE = 128 // GY
NN = (((1,), (0,)), ((), ()))
NT = (((1,), (1,)), ((), ()))


def dot(a, b, dims=NN):
    return lax.dot_general(a, b, dims, precision=HIGH, preferred_element_type=F32)


def bdot(a, b):
    return lax.dot_general(a, b, NN, preferred_element_type=F32)


def split(a):
    high = a.astype(BF16)
    return high, (a - high.astype(F32)).astype(BF16)


def swap(a):
    return pltpu.roll(a, 64, 1)


def lower_lanes(shape):
    return lax.broadcasted_iota(jnp.int32, shape, 1) < 64


def fold(m):
    return m[:64] + swap(m[64:])


def pair_up(s):
    return jnp.where(lower_lanes((32, 128)), s[:32], swap(s[32:]))


def unpair(p):
    return jnp.concatenate([p, swap(p)], axis=0)


def twice(s):
    low = lower_lanes((64, 128))
    zero = jnp.zeros_like(s)
    return jnp.concatenate([jnp.where(low, s, zero), jnp.where(low, zero, swap(s))], axis=0)


def inverse_factor(gram):
    lane = lax.broadcasted_iota(jnp.int32, (8, 128), 1)
    row = lax.broadcasted_iota(jnp.int32, (8, 128), 0)
    tiles = []
    for b in range(8):
        unit = jnp.where(lane == row + (64 + 8 * b), 1.0, 0.0)
        tiles.append(jnp.where(lane < 64, gram[8 * b : 8 * b + 8], unit))
    wide = lambda a: jnp.broadcast_to(a, (8, 128))
    for k in range(0, 64, STEP):
        own, at = divmod(k, 8)
        lines = [wide(tiles[own][at + j : at + j + 1]) for j in range(STEP)]
        cols = [[wide(t[:, k + j : k + j + 1]) for t in tiles[own:]] for j in range(STEP)]
        entry = [[wide(cols[j][0][at + n : at + n + 1]) if n >= j else None for n in range(STEP)] for j in range(STEP)]
        for j in range(STEP):
            inverse = 1.0 / entry[j][j]
            for n in range(j + 1, STEP):
                ratio = entry[j][n] * inverse
                for i in range(n, STEP):
                    entry[n][i] = entry[n][i] - ratio * entry[j][i]
                lines[n] = lines[n] - ratio * lines[j]
                cols[n] = [c - ratio * d for c, d in zip(cols[n], cols[j])]
            scaled = lines[j] * inverse
            for b in range(own, 8):
                col = cols[j][b - own]
                if b == own:
                    col = jnp.where(row > at + j, col, 0.0)
                tiles[b] = tiles[b] - col * scaled
    out = []
    for b in range(8):
        diag = jnp.sum(jnp.where(lane == row + 8 * b, tiles[b], 0.0), axis=1, keepdims=True)
        out.append(tiles[b] * lax.rsqrt(diag))
    return swap(jnp.concatenate(out, axis=0))


def kernel(
    field_hbm, m2_hbm, m3_hbm, start_hbm, out_ref,
    field, m2, m3, start,
    part, r1, r2, r3, pair, left_out, left_in, image, share_in, share, full, basis, lead, lead_in, lead_gx, lead_gy, lead_all,
    lead_send, lead_recv, in_sem, small_sem, ring_send, ring_recv, x_send, x_recv, s_send, s_recv, g_send, g_recv,
):
    mx = lax.axis_index("gx")
    my = lax.axis_index("gy")

    small = [
        pltpu.make_async_copy(src, dst, small_sem.at[n])
        for n, (src, dst) in enumerate(((m2_hbm, m2), (m3_hbm, m3), (start_hbm, start)))
    ]
    def load(c, h):
        at = pl.ds(pl.multiple_of(h * PACKED + c * HALF, HALF), HALF)
        return pltpu.make_async_copy(field_hbm.at[:, at, :], field.at[:, at, :], in_sem.at[c, h])

    small[0].start()
    small[1].start()
    for c in range(CHUNKS):
        for h in range(2):
            load(c, h).start()
    small[2].start()

    px, py = my // SIDE, lax.rem(my, SIDE)
    barrier = pltpu.get_barrier_semaphore()

    @pl.loop(1, GY, unroll=True)
    def _(r):
        pl.semaphore_signal(barrier, inc=1, device_id={"gy": lax.rem(my + r, GY)}, device_id_type=MESH)

    @pl.loop(1, GX, unroll=True)
    def _(r):
        pl.semaphore_signal(barrier, inc=1, device_id={"gx": lax.rem(mx + r, GX)}, device_id_type=MESH)

    small[0].wait()
    small[1].wait()
    m2h, m2l = split(jnp.transpose(m2[...]))
    right = jnp.concatenate([m2h, m2l], axis=1)
    tall = jnp.where(
        lax.broadcasted_iota(jnp.int32, (128, R3), 0) // 8 == lax.broadcasted_iota(jnp.int32, (128, R3), 1), 1.0, 0.0
    )
    wide = jnp.where(
        lax.broadcasted_iota(jnp.int32, (T3, 256), 0) == lax.broadcasted_iota(jnp.int32, (T3, 256), 1) // 8, 1.0, 0.0
    )
    same = (
        lax.broadcasted_iota(jnp.int32, (128, 256), 0) % 8 == lax.broadcasted_iota(jnp.int32, (128, 256), 1) % 8
    )
    wh, wl = (
        jnp.where(same, bdot(bdot(tall.astype(BF16), piece).astype(BF16), wide.astype(BF16)), 0.0).astype(BF16)
        for piece in split(m3[...])
    )
    w2 = jnp.concatenate([wh, wl], axis=0)
    low = lower_lanes((256, 128))
    low64 = lower_lanes((64, 128))

    def project(i0):
        tile = field[:, pl.ds(i0, 8), :].reshape(T3 * 8, COLS)
        th, tl = split(tile)
        return bdot(th, right) + bdot(tl, right)

    def compute(c):
        pairs = []
        for h in range(2):
            load(c, h).wait()
        for n in range(HALF // 8):
            i0 = pl.multiple_of(c * HALF + n * 8, 8)
            a, b = project(i0), project(i0 + PACKED)
            pairs.append(jnp.where(low, a + swap(a), b + swap(b)))
        blocks = []
        for n in range(0, HALF // 8, 2):
            bh, bl = split(jnp.concatenate(pairs[n : n + 2], axis=1))
            two = bdot(w2, bh)
            res = two[:128] + two[128:] + bdot(wh, bl)
            blocks += [res[:, :128].reshape(R3, 8, 128), res[:, 128:].reshape(R3, 8, 128)]
        return blocks

    first, second = (px, py), (py, px)

    def near(half, phase, step):
        if (half + phase) % 2 == 0:
            return {"gy": lax.rem(px + step + SIDE, SIDE) * SIDE + py}
        return {"gy": px * SIDE + lax.rem(py + step + SIDE, SIDE)}

    def send(src, dst, stage, c, half, phase, step):
        pltpu.make_async_remote_copy(
            src, dst.at[c, half, (1 - step) // 2], ring_send.at[stage], ring_recv.at[stage, c],
            device_id=near(half, phase, step), device_id_type=MESH,
        ).start()

    def arrive(dst, stage, c):
        pltpu.make_async_copy(dst.at[c], dst.at[c], ring_recv.at[stage, c]).wait()

    def hop(at, step):
        return lax.rem(at + step + SIDE, SIDE)

    def stage1(c):
        for half in range(2):
            far = hop(first[half], 2)
            for step in (1, -1):
                send(part.at[c, half, far, pl.ds(1 - step, 2)], r1, 0, c, half, 0, step)

    def stage2(c):
        arrive(r1, 0, c)
        for half in range(2):
            for step in (1, -1):
                to = hop(first[half], step)
                at = pl.ds(1 - step, 2)
                part[c, half, to, at] = part[c, half, to, at] + r1[c, half, (1 - step) // 2]
                send(part.at[c, half, to], r2, 1, c, half, 0, step)

    def stage3(c):
        arrive(r2, 1, c)
        for half in range(2):
            me = first[half]
            part[c, half, me] = part[c, half, me] + r2[c, half, 0] + r2[c, half, 1]
            for step in range(1, SIDE):
                to = hop(second[half], step)
                pltpu.make_async_remote_copy(
                    part.at[c, half, me, to], r3.at[c, half, step - 1], ring_send.at[2], ring_recv.at[2, c],
                    device_id=near(half, 1, step), device_id_type=MESH,
                ).start()

    def stage4(c):
        arrive(r3, 2, c)
        for half in range(2):
            at = pl.ds(pl.multiple_of(c * HALF + half * 16, 16), 16)
            total = part[c, half, first[half], second[half]]
            for step in range(1, SIDE):
                total = total + r3[c, half, step - 1]
            pair[at] = total

    stages = (stage2, stage3, stage4)

    def fill(c):
        blocks = compute(c)
        for n in range(2):
            at = slice(8 * n, 8 * n + 8)
            part[c, 0, :, :, at] = blocks[n].reshape(SIDE, SIDE, 8, 128)
            square = blocks[2 + n].reshape(SIDE, SIDE, 8, 128)
            for k in range(SIDE):
                part[c, 1, :, k, at] = square[k]

    def lead_part():
        bh, bl = basis[0], basis[1]
        both = jnp.concatenate([bh, bl], axis=0)

        def rows(x, y):
            return jnp.stack([part[:, 0, x, y], part[:, 1, y, x]], axis=1).reshape(PACKED, 128)

        for s in range(R3 // 2):
            x, y = divmod(s, SIDE)
            uh, ul = split(jnp.concatenate([rows(x, y), rows(x + 2, y)], axis=1))
            two = bdot(both, uh)
            m = two[:128] + two[128:] + bdot(bh, ul)
            value = jnp.where(low64, m[:64, :128] + swap(m[64:, :128]), m[64:, 128:] + swap(m[:64, 128:]))
            value = value.reshape(8, 8, 128)
            lead[:, s] = value

    def lead_stage1():
        @pl.loop(1, GX, unroll=True)
        def _(r):
            dest = lax.rem(mx + r, GX)
            pltpu.make_async_remote_copy(
                lead.at[dest], lead_in.at[r - 1], lead_send.at[0], lead_recv.at[0],
                device_id={"gx": dest}, device_id_type=MESH,
            ).start()

    def lead_stage2():
        pltpu.make_async_copy(lead_in, lead_in, lead_recv.at[0]).wait()
        total = lead[mx]
        for r in range(GX - 1):
            total = total + lead_in[r]
        lead_gx[...] = total

        @pl.loop(1, GY, unroll=True)
        def _(r):
            dest = lax.rem(my + r, GY)
            pltpu.make_async_remote_copy(
                lead_gx.at[lax.rem(dest, 8)], lead_gy.at[r - 1], lead_send.at[1], lead_recv.at[1],
                device_id={"gy": dest}, device_id_type=MESH,
            ).start()

    def lead_stage3():
        pltpu.make_async_copy(lead_gy, lead_gy, lead_recv.at[1]).wait()
        total = lead_gx[lax.rem(my, 8)]
        for r in range(GY - 1):
            total = total + lead_gy[r]
        lead_all[mx] = jnp.where(my < 8, total, swap(total))

        @pl.loop(1, GX, unroll=True)
        def _(r):
            pltpu.make_async_remote_copy(
                lead_all.at[mx], lead_all.at[mx], lead_send.at[2], lead_recv.at[2],
                device_id={"gx": lax.rem(mx + r, GX)}, device_id_type=MESH,
            ).start()

    @pl.loop(0, EARLY)
    def _(c):
        fill(c)

    small[2].wait()
    for h in range(2):
        for n, piece in enumerate(split(start[:, h * PACKED : h * PACKED + PACKED])):
            basis[n, 64 * h : 64 * h + 64] = piece

    pl.semaphore_wait(barrier, GX + GY - 2)

    @pl.loop(0, EARLY)
    def _(c):
        stage1(c)

    @pl.loop(EARLY, RING)
    def _(c):
        fill(c)
        stage1(c)

        for n, stage in enumerate(stages):
            @pl.when(c >= LAG * (n + 1))
            def _(n=n, stage=stage):
                stage(c - LAG * (n + 1))

    lead_part()
    lead_stage1()

    @pl.loop(RING, RING + 3 * LAG)
    def _(c):
        @pl.when(c == RING + SECOND)
        def _():
            lead_stage2()

        @pl.when(c == RING + THIRD)
        def _():
            lead_stage3()

        for n, stage in enumerate(stages):
            at = c - LAG * (n + 1)

            @pl.when((at >= 0) & (at < RING))
            def _(at=at, stage=stage):
                stage(at)

    def sum_over_gx(n, value):
        left_out[n] = value

        @pl.loop(1, GX, unroll=True)
        def _(r):
            pltpu.make_async_remote_copy(
                left_out.at[n], left_in.at[n, r - 1], x_send.at[n], x_recv.at[n],
                device_id={"gx": lax.rem(mx + r, GX)}, device_id_type=MESH,
            ).start()

        def finish():
            pltpu.make_async_copy(left_in.at[n], left_in.at[n], x_recv.at[n]).wait()
            total = value
            for r in range(GX - 1):
                total = total + left_in[n, r]
            return unpair(total)

        return finish, lambda: pltpu.make_async_copy(left_in.at[n], left_in.at[n], x_send.at[n]).wait()

    def sum_over_gy(n, value, beside):
        image[n] = value

        @pl.loop(1, GY, unroll=True)
        def _(r):
            dest = lax.rem(my + r, GY)
            pltpu.make_async_remote_copy(
                image.at[n, pl.ds(pl.multiple_of(dest * SHARE, SHARE), SHARE)], share_in.at[n, r - 1],
                s_send.at[n], s_recv.at[n], device_id={"gy": dest}, device_id_type=MESH,
            ).start()

        pltpu.make_async_copy(share_in.at[n], share_in.at[n], s_recv.at[n]).wait()
        total = image[n, pl.ds(pl.multiple_of(my * SHARE, SHARE), SHARE)]
        for r in range(GY - 1):
            total = total + share_in[n, r]
        share[n] = total
        full[n, my] = total

        @pl.loop(1, GY, unroll=True)
        def _(r):
            pltpu.make_async_remote_copy(
                share.at[n], full.at[n, my], g_send.at[n], g_recv.at[n],
                device_id={"gy": lax.rem(my + r, GY)}, device_id_type=MESH,
            ).start()

        aside = beside()
        pltpu.make_async_copy(share_in.at[n], share_in.at[n], g_recv.at[n]).wait()

        def end():
            pltpu.make_async_copy(share_in.at[n], share_in.at[n], s_send.at[n]).wait()
            pltpu.make_async_copy(share_in.at[n], share_in.at[n], g_send.at[n]).wait()

        return full[n].reshape(128, PACKED), aside, end

    uh, ul = split(pair[...])

    def times_units(a, dims):
        ah, al = split(a)
        three = functools.partial(lax.dot_general, dimension_numbers=dims, preferred_element_type=F32)
        two = three(jnp.concatenate([ah, al], axis=0), uh)
        return two[:128] + two[128:] + three(ah, ul)

    pltpu.make_async_copy(lead_all.at[pl.ds(0, 7)], lead_all.at[pl.ds(0, 7)], lead_recv.at[2]).wait()
    image1, _, end1 = sum_over_gy(0, times_units(twice(lead_all[...].reshape(64, 128)), NT), lambda: None)
    finish_left, end2 = sum_over_gx(0, pair_up(fold(times_units(image1, NN))))
    finish_gram, end5 = sum_over_gx(2, pair_up(fold(dot(image1, image1, NT))))
    raw, factor, end3 = sum_over_gy(
        1, times_units(twice(finish_left()), NT), lambda: inverse_factor(finish_gram())
    )
    image2 = dot(twice(factor), raw)
    finish_gram, end4 = sum_over_gx(1, pair_up(fold(dot(image2, image2, NT))))
    factor = inverse_factor(finish_gram())
    final = dot(twice(factor), image2) * jnp.sqrt(F32(ROWS * GX))
    out_ref[:, :PACKED] = final[:64]
    out_ref[:, PACKED:] = final[64:]
    for n, ref in enumerate((r1, r2, r3)):
        pltpu.make_async_copy(ref, ref, ring_send.at[n]).wait()
    for n, ref in enumerate((lead_in, lead_gy, lead_all.at[pl.ds(0, 7)])):
        pltpu.make_async_copy(ref, ref, lead_send.at[n]).wait()
    for end in (end1, end2, end3, end4, end5):
        end()


def on_device(field, mode2_factor, mode3_factor, start_factor):
    dma = pltpu.SemaphoreType.DMA
    out = pl.pallas_call(
        kernel,
        out_shape=jax.ShapeDtypeStruct((RANK, ROWS), F32),
        in_specs=[pl.BlockSpec(memory_space=pl.ANY)] * 4,
        out_specs=pl.BlockSpec(memory_space=pltpu.VMEM),
        scratch_shapes=[
            pltpu.VMEM((T3, ROWS, COLS), F32),
            pltpu.VMEM((RANK, COLS), F32),
            pltpu.VMEM((R3, T3), F32),
            pltpu.VMEM((RANK, ROWS), F32),
            pltpu.VMEM((RING, 2, SIDE, SIDE, 16, 128), F32),
            pltpu.VMEM((RING, 2, 2, 2, 16, 128), F32),
            pltpu.VMEM((RING, 2, 2, SIDE, 16, 128), F32),
            pltpu.VMEM((RING, 2, SIDE - 1, 16, 128), F32),
            pltpu.VMEM((PACKED, 128), F32),
            pltpu.VMEM((3, 32, 128), F32),
            pltpu.VMEM((3, GX - 1, 32, 128), F32),
            pltpu.VMEM((2, 128, PACKED), F32),
            pltpu.VMEM((2, GY - 1, SHARE, PACKED), F32),
            pltpu.VMEM((2, SHARE, PACKED), F32),
            pltpu.VMEM((2, GY, SHARE, PACKED), F32),
            pltpu.VMEM((2, 128, PACKED), BF16),
            pltpu.VMEM((GX, 8, 8, 128), F32),
            pltpu.VMEM((GX - 1, 8, 8, 128), F32),
            pltpu.VMEM((8, 8, 128), F32),
            pltpu.VMEM((GY - 1, 8, 128), F32),
            pltpu.VMEM((GX, 8, 128), F32),
            dma((3,)), dma((3,)),
            dma((CHUNKS, 2)),
            dma((3,)),
            dma((3,)), dma((3, RING)),
            dma((3,)), dma((3,)),
            dma((2,)), dma((2,)),
            dma((2,)), dma((2,)),
        ],
        compiler_params=pltpu.CompilerParams(
            collective_id=0, has_side_effects=True, vmem_limit_bytes=60 * 1024 * 1024
        ),
    )(field, mode2_factor.T, mode3_factor.T, start_factor.T)
    return out.T


def solution(mesh):
    placed = (P(None, "gx", "gy"), P("gy", None), P(), P("gx", None))
    return jax.shard_map(
        on_device, mesh=mesh, in_specs=placed, out_specs=P("gx", None), check_vma=False
    )
```
